32 devices in a mesh: rcv: 8 (over z, core), twin: 4 (over y, x).
Axes of the slice: x: 2, y: 2, z: 4, core: 2. Of those that a mesh axis runs over, the one named last changes fastest.
Arguments:
- record: bfloat16 [2048, 8, 2048], P('rcv', None, 'twin'), may hold values from -6 to 6
- slip_block: int32 [16], P('twin'), may hold values from 4 to 31, as said below
- ghost_lag: int32 [16, 4], P('twin'), may hold values from 1 to 35, as said below
- order_ops: bfloat16 [4, 512, 512], replicated, may hold values from -0.25 to 0.25
Outputs:
- denoised: bfloat16 [2048, 8, 2048], P('rcv', None, 'twin')
The draws below stay inside these ranges and needn't reach their ends.
Inputs may be any that keep to these rules, and one draw needn't show every extreme that they name: `slip_block`: record r begins in a block b with b mod 4 = r // 4 and b // 4 >= 1; the 4 records of one twin index begin in distinct blocks. `ghost_lag`: among the records of one twin index, at most 5 pairs (r, h) with landing >= 0 land on blocks of one twin index; some twin index receives exactly 5 such pairs from every twin index.
All inputs are finite; a program needn't handle non-finite values.
Results may differ from the reference program's by a relative error of at most 0.009.
Values may be sent and summed in bfloat16 or wider, within the bound.
A program may use at most 128 MiB of HBM per device.

```python
import jax
import jax.numpy as jnp
from jax import lax

PB = 512
NORD = 4
ROUNDS = 8
REC_DEV = 4
CH = 2048
NBLK = 32
NREC = 16
CAP = 5
N_TWIN = 4


def routing_tables(key):
    twin_count = NREC // REC_DEV
    pair_total = REC_DEV * NORD
    base = jax.random.fold_in(key, 811)
    keys = jax.random.split(base, 5)
    hot = jax.random.randint(keys[0], (), 0, twin_count)
    round_scores = jax.random.randint(keys[1], (twin_count, ROUNDS - 1), 0, 1 << 20) * (ROUNDS - 1) + jnp.arange(ROUNDS - 1)
    slip_round = jnp.argsort(round_scores, axis=1)[:, :REC_DEV] + 1
    device = jnp.arange(twin_count)[:, None]
    slip = slip_round * twin_count + device
    pair_scores = jax.random.randint(keys[2], (twin_count, pair_total), 0, 1 << 20) * pair_total + jnp.arange(pair_total)
    rank = jnp.argsort(jnp.argsort(pair_scores, axis=1), axis=1)
    other_scores = jax.random.randint(keys[3], (twin_count, twin_count - 1), 0, 1 << 20) * (twin_count - 1) + jnp.arange(twin_count - 1)
    others = (hot + 1 + jnp.argsort(other_scores, axis=1)) % twin_count
    later = jnp.maximum(rank - CAP, 0) % (twin_count - 1)
    dest_dev = jnp.where(rank < CAP, hot, jnp.take_along_axis(others, later, axis=1))
    pair_round = jnp.repeat(slip_round, NORD, axis=1)
    pair_slip = jnp.repeat(slip, NORD, axis=1)
    lowest = jnp.where(rank < CAP, 0, -1)
    dest_round = jax.random.randint(keys[4], (twin_count, pair_total), lowest, pair_round)
    lag = pair_slip - (dest_round * twin_count + dest_dev)
    forced = (device == twin_count - 1) & (rank == pair_total - 1)
    lag = jnp.where(forced, (ROUNDS + 1) * twin_count - 1, lag)
    return (slip.reshape(NREC).astype(jnp.int32), lag.reshape(NREC, NORD).astype(jnp.int32))


def draw_slip_block(key, part):
    return routing_tables(key)[0]


def draw_ghost_lag(key, part):
    return routing_tables(key)[1]


def level_of(own_key, extent, cuts, smallest, largest):
    def one(axis_at, shards_of):
        steps = jax.random.uniform(jax.random.fold_in(jax.random.fold_in(own_key, 6), axis_at), (shards_of,), jnp.float32, smallest / len(cuts), largest / len(cuts))
        return jnp.repeat(jnp.exp(steps), extent[axis_at] // shards_of).reshape((-1,) + (1,) * (len(extent) - axis_at - 1))

    level = one(*cuts[0])
    for cut in cuts[1:]:
        level = level * one(*cut)
    return level


def normal_values(own_key, dims, deviation, most, cuts=(), held_as=jnp.bfloat16):
    factor_of = level_of(own_key, dims, cuts, -0.22, 0.18) if cuts else 1.0
    drawn = jax.random.normal(own_key, dims, jnp.float32) * deviation * factor_of
    return jnp.minimum(jnp.maximum(drawn, -most), most).astype(held_as)


def setup_inputs(seed: int = 0) -> dict:
    key_list = jax.random.split(jax.random.key(seed), 5)
    return {
        "record": normal_values(key_list[0], (CH, ROUNDS, N_TWIN * PB), 1.0, 6.0, ((0, 8), (2, 4))),
        "slip_block": draw_slip_block(jax.random.fold_in(key_list[4], 71), 0),
        "ghost_lag": draw_ghost_lag(jax.random.fold_in(key_list[4], 71), 0),
        "order_ops": normal_values(key_list[3], (NORD, PB, PB), PB ** -0.5, 0.25),
    }


def reference(record, slip_block, ghost_lag, order_ops):
    channels = record.shape[0]
    blocks = record.reshape(channels, NBLK, PB)
    pair_total = NREC * NORD

    def add_pair(noise, index):
        rec_index = index // NORD
        order_index = index % NORD
        slip = slip_block[rec_index].astype(jnp.int32)
        target = (slip - ghost_lag[rec_index, order_index]).astype(jnp.int32)
        guide = lax.dynamic_slice_in_dim(blocks, slip, 1, 1)[:, 0, :]
        operator = lax.dynamic_index_in_dim(order_ops, order_index, 0, keepdims=False)
        estimate = jnp.dot(guide, operator, preferred_element_type=jnp.float32)
        estimate = lax.optimization_barrier(estimate.astype(jnp.bfloat16)).astype(jnp.float32)
        place = jnp.maximum(target, 0).astype(jnp.int32)
        current = lax.dynamic_slice_in_dim(noise, place, 1, 1)
        update = current + jnp.where(target >= 0, estimate, jnp.zeros_like(estimate))[:, None, :]
        return lax.dynamic_update_slice_in_dim(noise, update, place, 1), None

    start = jnp.zeros((channels, NBLK, PB), jnp.float32)
    noise, _ = lax.scan(add_pair, start, jnp.arange(pair_total, dtype=jnp.int32))
    cleaned = lax.optimization_barrier((blocks.astype(jnp.float32) - noise).astype(jnp.bfloat16)).astype(jnp.float32)
    padded = jnp.pad(cleaned, ((1, 1), (0, 0), (0, 0)))
    smooth = 0.5 * cleaned + 0.25 * (padded[:-2] + padded[2:])
    return smooth.astype(jnp.bfloat16).reshape(channels, ROUNDS, N_TWIN * PB)
```

```python
import functools

import jax
import jax.numpy as jnp
from jax import lax
from jax.experimental import pallas as pl
from jax.experimental.pallas import tpu as pltpu
from jax.sharding import PartitionSpec as P

MESH = pl.DeviceIdType.MESH
GROUP = 16
STEPS = 4
F32, BF16 = jnp.float32, jnp.bfloat16


def iota(shape, dim):
    return lax.broadcasted_iota(jnp.int32, shape, dim)


def clean_kernel(
    twins, lines, slip_ref, lag_ref, rec_ref, ops_hbm, out_ref,
    guides, lands, picks, spread, ops_ref, edges,
    ops_sem, land_send, land_recv, send_sem, recv_sem, edge_send, edge_recv,
):
    me = lax.axis_index("twin")
    line = lax.axis_index("rcv")
    recs, orders = lag_ref.shape
    rows, samples = rec_ref.shape
    groups, held, _ = guides.shape
    mine = held // twins
    rounds = rows // (groups * GROUP)
    block = GROUP * rounds
    per = groups // STEPS

    load_ops = pltpu.make_async_copy(ops_hbm, ops_ref, ops_sem)
    load_ops.start()

    others = [lax.rem(me + d, twins) for d in range(1, twins)]
    left, right = lax.rem(line + lines - 1, lines), lax.rem(line + 1, lines)
    barrier = pltpu.get_barrier_semaphore()
    for other in others:
        pl.semaphore_signal(barrier, inc=1, device_id={"twin": other}, device_id_type=MESH)
    for other in (left, right):
        pl.semaphore_signal(barrier, inc=1, device_id={"rcv": other}, device_id_type=MESH)

    order_row, rec_lane = iota((8, 128), 0), (iota((8, 128), 1) // GROUP) % recs
    land = jnp.full((8, 128), -1, jnp.int32)
    for r in range(recs):
        for h in range(orders):
            here = (order_row == h) & (rec_lane == r)
            land = jnp.where(here, slip_ref[r] - lag_ref[r, h], land)
    lands[me] = land

    row, col = iota((mine, block), 0), iota((mine, block), 1)
    slip = jnp.zeros((mine, block), jnp.int32)
    for r in range(recs):
        slip = jnp.where(row // GROUP == r, slip_ref[r], slip)
    pick = (row % GROUP == col // rounds) & ((col % rounds) * twins + me == slip)
    pick = jnp.where(pick, 1.0, 0.0).astype(BF16)

    def chunk(step):
        return lax.rem(step * (STEPS - 1), STEPS)

    def own(twin):
        return pl.ds(pl.multiple_of(twin * mine, mine), mine)

    def move(step, begin, count, twin, to, index):
        part = guides.at[pl.ds(chunk(step) * per + begin, count), own(twin)]
        return pltpu.make_async_remote_copy(
            src_ref=part, dst_ref=part, send_sem=send_sem.at[step, index],
            recv_sem=recv_sem.at[step, index], device_id={"twin": to}, device_id_type=MESH,
        )

    def extract(step):
        def one(i, _):
            g = chunk(step) * per + i
            rec = rec_ref[pl.ds(pl.multiple_of(g * block, block), block), :]
            guide = jnp.dot(pick, rec, preferred_element_type=F32)
            guides[g, own(me), :] = guide.astype(BF16)
            return 0
        lax.fori_loop(0, per, one, 0)

    relay = twins == 4
    if relay:
        across = (me // 2) * 2 + (1 - me % 2)
        along = (1 - me // 2) * 2 + me % 2
        half = per // 2

    def first_copies(step):
        if relay:
            return [move(step, 0, per, me, across, 0), move(step, 0, per, me, along, 1)]
        return [move(step, 0, per, me, other, d) for d, other in enumerate(others)]

    def relays(step):
        return [
            move(step, 0, half, along, across, 2),
            move(step, half, per - half, across, along, 3),
        ]

    extract(0)
    pl.semaphore_wait(barrier, twins + 1)
    for copy in first_copies(0):
        copy.start()

    def land_copy(d):
        return pltpu.make_async_remote_copy(
            src_ref=lands.at[me], dst_ref=lands.at[me], send_sem=land_send.at[d],
            recv_sem=land_recv.at[d], device_id={"twin": others[d]}, device_id_type=MESH,
        )

    for d in range(twins - 1):
        land_copy(d).start()

    def send_rest(step, _):
        extract(step)
        for copy in first_copies(step):
            copy.start()
        return 0

    lax.fori_loop(1, STEPS, send_rest, 0)

    for d in range(twins - 1):
        land_copy(d).wait()

    row, col = iota((block, 128), 0), iota((block, 128), 1)
    same = row // rounds == col % GROUP
    goal = (row % rounds) * twins + me
    per_tile = 128 // mine
    for tile in range(held // 128):
        for h in range(orders):
            got = lands[tile * per_tile, h : h + 1, :]
            got = jnp.broadcast_to(got, (block, 128))
            for k in range(1, per_tile):
                more = lands[tile * per_tile + k, h : h + 1, :]
                got = jnp.where(col // mine == k, jnp.broadcast_to(more, (block, 128)), got)
            hit = jnp.where(same & (got == goal), 1.0, 0.0).astype(BF16)
            picks[h * block : (h + 1) * block, tile * 128 : (tile + 1) * 128] = hit
    load_ops.wait()

    pad = 2 * rounds

    def work(step):
        def one(i, _):
            for k in range(2):
                g = chunk(step) * per + i * 2 + k
                landed = jnp.dot(picks[...], guides[g], preferred_element_type=F32).astype(BF16)
                for h in range(orders):
                    spread[k * block : (k + 1) * block, h * samples : (h + 1) * samples] = landed[
                        h * block : (h + 1) * block
                    ]
            noise = jnp.dot(spread[...], ops_ref[...], preferred_element_type=F32)
            at = (chunk(step) * per + i * 2) * block
            at = pl.multiple_of(at, 2 * block)
            rec = rec_ref[pl.ds(at, 2 * block), :].astype(F32)
            out_ref[pl.ds(pl.multiple_of(at + pad, pad), 2 * block), :] = (rec - noise).astype(BF16)
            return 0
        lax.fori_loop(0, per // 2, one, 0)

    def arrive(step):
        if relay:
            for copy in first_copies(step):
                copy.wait_recv()
            for copy in relays(step):
                copy.start()

    def finish(step):
        for copy in relays(step) if relay else first_copies(step):
            copy.wait_recv()

    def edge_copies():
        return [
            pltpu.make_async_remote_copy(
                src_ref=edges.at[k], dst_ref=edges.at[2 + k], send_sem=edge_send.at[k],
                recv_sem=edge_recv.at[k], device_id={"rcv": to}, device_id_type=MESH,
            )
            for k, to in enumerate((left, right))
        ]

    def advance(step, _):
        arrive(step + 1)
        finish(step)
        work(step)
        return 0

    arrive(0)
    lax.fori_loop(0, 2, advance, 0)
    edges[0] = out_ref[pad : 2 * pad, :]
    edges[1] = out_ref[rows : rows + pad, :]
    for copy in edge_copies():
        copy.start()
    lax.fori_loop(2, STEPS - 1, advance, 0)
    finish(STEPS - 1)
    work(STEPS - 1)

    for copy in edge_copies():
        copy.wait()
    zero = jnp.zeros((pad, samples), BF16)
    out_ref[0:pad, :] = jnp.where(line > 0, edges[3], zero)
    out_ref[rows + pad : rows + 2 * pad, :] = jnp.where(line < lines - 1, edges[2], zero)

    def sent(step, _):
        for copy in first_copies(step) + (relays(step) if relay else []):
            copy.wait_send()
        return 0

    lax.fori_loop(0, STEPS, sent, 0)


def local(record, slip_block, ghost_lag, order_ops):
    twins, lines = lax.axis_size("twin"), lax.axis_size("rcv")
    channels, rounds, samples = record.shape
    recs, orders = ghost_lag.shape
    groups, mine = channels // GROUP, recs * GROUP
    block = GROUP * rounds
    ways = max(twins, 4)
    vmem = pl.BlockSpec(memory_space=pltpu.VMEM)
    smem = pl.BlockSpec(memory_space=pltpu.SMEM)
    padded = pl.pallas_call(
        functools.partial(clean_kernel, twins, lines),
        out_shape=jax.ShapeDtypeStruct(((channels + 4) * rounds, samples), BF16),
        in_specs=[smem, smem, vmem, pl.BlockSpec(memory_space=pl.ANY)],
        out_specs=vmem,
        scratch_shapes=[
            pltpu.VMEM((groups, twins * mine, samples), BF16),
            pltpu.VMEM((twins, 8, 128), jnp.int32),
            pltpu.VMEM((orders * block, twins * mine), BF16),
            pltpu.VMEM((2 * block, orders * samples), BF16),
            pltpu.VMEM((orders * samples, samples), BF16),
            pltpu.VMEM((4, 2 * rounds, samples), BF16),
            pltpu.SemaphoreType.DMA,
            pltpu.SemaphoreType.DMA((twins,)),
            pltpu.SemaphoreType.DMA((twins,)),
            pltpu.SemaphoreType.DMA((STEPS, ways)),
            pltpu.SemaphoreType.DMA((STEPS, ways)),
            pltpu.SemaphoreType.DMA((2,)),
            pltpu.SemaphoreType.DMA((2,)),
        ],
        compiler_params=pltpu.CompilerParams(
            collective_id=0, has_side_effects=True, vmem_limit_bytes=48 * 2**20
        ),
        cost_estimate=pl.CostEstimate(
            flops=7 * 10**9, bytes_accessed=6 * 2**20, transcendentals=0
        ),
    )(
        slip_block, ghost_lag, record.reshape(channels * rounds, samples),
        order_ops.reshape(orders * samples, samples),
    )
    wide = padded.reshape(channels + 4, rounds, samples).astype(F32)
    middle = wide[2 : channels + 2]
    smooth = 0.5 * middle + 0.25 * (wide[1 : channels + 1] + wide[3 : channels + 3])
    return smooth.astype(BF16)


def solution(mesh):
    placed = (P("rcv", None, "twin"), P("twin"), P("twin", None), P())
    return jax.shard_map(
        local, mesh=mesh, in_specs=placed, out_specs=P("rcv", None, "twin"), check_vma=False
    )
```

```python
import functools

import jax
import jax.numpy as jnp
from jax import lax
from jax.experimental import pallas as pl
from jax.experimental.pallas import tpu as pltpu
from jax.sharding import PartitionSpec as P

MESH = pl.DeviceIdType.MESH
GROUP = 16
STEPS = 8
AHEAD = 3
F32, BF16 = jnp.float32, jnp.bfloat16


def iota(shape, dim):
    return lax.broadcasted_iota(jnp.int32, shape, dim)


def clean_kernel(
    twins, lines, slip_hbm, lag_hbm, rec_hbm, ops_hbm, out_hbm,
    slip_ref, lag_ref, rec_ref, ops_ref, out_ref,
    guides, lands, picks, spread, edges,
    small_sem, rec_sem, out_sem, land_send, land_recv, send_sem, recv_sem, edge_send, edge_recv,
):
    me = lax.axis_index("twin")
    line = lax.axis_index("rcv")
    recs, orders = lag_ref.shape
    rows, samples = rec_ref.shape
    groups, held, _ = guides.shape
    mine = held // twins
    rounds = rows // (groups * GROUP)
    block = GROUP * rounds
    per = groups // STEPS

    def chunk(step):
        return lax.rem(step * (STEPS - 1), STEPS)

    size = rows // STEPS

    def load(step):
        part = pl.ds(pl.multiple_of(chunk(step) * size, size), size)
        return pltpu.make_async_copy(rec_hbm.at[part], rec_ref.at[part], rec_sem.at[step])

    load_slip = pltpu.make_async_copy(slip_hbm, slip_ref, small_sem.at[0])
    load_lag = pltpu.make_async_copy(lag_hbm, lag_ref, small_sem.at[1])
    load_ops = pltpu.make_async_copy(ops_hbm, ops_ref, small_sem.at[2])
    load_slip.start()
    load_lag.start()
    for step in range(STEPS):
        load(step).start()
    load_ops.start()

    others = [lax.rem(me + d, twins) for d in range(1, twins)]
    left, right = lax.rem(line + lines - 1, lines), lax.rem(line + 1, lines)
    barrier = pltpu.get_barrier_semaphore()
    for other in others:
        pl.semaphore_signal(barrier, inc=1, device_id={"twin": other}, device_id_type=MESH)
    for other in (left, right):
        pl.semaphore_signal(barrier, inc=1, device_id={"rcv": other}, device_id_type=MESH)

    load_slip.wait()
    load_lag.wait()

    order_row, rec_lane = iota((8, 128), 0), (iota((8, 128), 1) // GROUP) % recs
    land = jnp.full((8, 128), -1, jnp.int32)
    for r in range(recs):
        for h in range(orders):
            here = (order_row == h) & (rec_lane == r)
            land = jnp.where(here, slip_ref[r] - lag_ref[r, h], land)
    lands[me] = land

    row, col = iota((mine, block), 0), iota((mine, block), 1)
    slip = jnp.zeros((mine, block), jnp.int32)
    for r in range(recs):
        slip = jnp.where(row // GROUP == r, slip_ref[r], slip)
    pick = (row % GROUP == col // rounds) & ((col % rounds) * twins + me == slip)
    pick = jnp.where(pick, 1.0, 0.0).astype(BF16)

    def own(twin):
        return pl.ds(pl.multiple_of(twin * mine, mine), mine)

    def move(step, begin, count, twin, to, index):
        part = guides.at[pl.ds(chunk(step) * per + begin, count), own(twin)]
        return pltpu.make_async_remote_copy(
            src_ref=part, dst_ref=part, send_sem=send_sem.at[step, index],
            recv_sem=recv_sem.at[step, index], device_id={"twin": to}, device_id_type=MESH,
        )

    def extract(step):
        load(step).wait()

        def one(i, _):
            g = chunk(step) * per + i
            rec = rec_ref[pl.ds(pl.multiple_of(g * block, block), block), :]
            guide = jnp.dot(pick, rec, preferred_element_type=F32)
            guides[g, own(me), :] = guide.astype(BF16)
            return 0
        lax.fori_loop(0, per, one, 0)

    relay = twins == 4
    if relay:
        across = (me // 2) * 2 + (1 - me % 2)
        along = (1 - me // 2) * 2 + me % 2
        half = per // 2

    def first_copies(step):
        if relay:
            return [move(step, 0, per, me, across, 0), move(step, 0, per, me, along, 1)]
        return [move(step, 0, per, me, other, d) for d, other in enumerate(others)]

    def relays(step):
        return [
            move(step, 0, half, along, across, 2),
            move(step, half, per - half, across, along, 3),
        ]

    extract(0)
    pl.semaphore_wait(barrier, twins + 1)
    for copy in first_copies(0):
        copy.start()

    def land_copy(d):
        return pltpu.make_async_remote_copy(
            src_ref=lands.at[me], dst_ref=lands.at[me], send_sem=land_send.at[d],
            recv_sem=land_recv.at[d], device_id={"twin": others[d]}, device_id_type=MESH,
        )

    for d in range(twins - 1):
        land_copy(d).start()

    def send_next(step, _):
        extract(step)
        for copy in first_copies(step):
            copy.start()
        return 0

    def extract_next(step, _):
        extract(step)
        return 0

    lax.fori_loop(1, AHEAD, send_next, 0)
    lax.fori_loop(AHEAD, STEPS, extract_next, 0)

    for d in range(twins - 1):
        land_copy(d).wait()

    row, col = iota((block, 128), 0), iota((block, 128), 1)
    same = row // rounds == col % GROUP
    goal = (row % rounds) * twins + me
    per_tile = 128 // mine
    for tile in range(held // 128):
        for h in range(orders):
            got = lands[tile * per_tile, h : h + 1, :]
            got = jnp.broadcast_to(got, (block, 128))
            for k in range(1, per_tile):
                more = lands[tile * per_tile + k, h : h + 1, :]
                got = jnp.where(col // mine == k, jnp.broadcast_to(more, (block, 128)), got)
            hit = jnp.where(same & (got == goal), 1.0, 0.0).astype(BF16)
            picks[h * block : (h + 1) * block, tile * 128 : (tile + 1) * 128] = hit
    load_ops.wait()

    pad = 2 * rounds

    def work(step):
        def one(i, _):
            for k in range(2):
                g = chunk(step) * per + i * 2 + k
                landed = jnp.dot(picks[...], guides[g], preferred_element_type=F32).astype(BF16)
                for h in range(orders):
                    spread[k * block : (k + 1) * block, h * samples : (h + 1) * samples] = landed[
                        h * block : (h + 1) * block
                    ]
            noise = jnp.dot(spread[...], ops_ref[...], preferred_element_type=F32)
            at = (chunk(step) * per + i * 2) * block
            at = pl.multiple_of(at, 2 * block)
            rec = rec_ref[pl.ds(at, 2 * block), :].astype(F32)
            out_ref[pl.ds(pl.multiple_of(at + pad, pad), 2 * block), :] = (rec - noise).astype(BF16)
            return 0
        lax.fori_loop(0, per // 2, one, 0)
        store(step).start()

    def store(step):
        part = pl.ds(pl.multiple_of(chunk(step) * size + pad, pad), size)
        return pltpu.make_async_copy(out_ref.at[part], out_hbm.at[part], out_sem.at[step])

    def arrive(step):
        if relay:
            for copy in first_copies(step):
                copy.wait_recv()
            for copy in relays(step):
                copy.start()

    def finish(step):
        for copy in relays(step) if relay else first_copies(step):
            copy.wait_recv()

    def edge_copies():
        return [
            pltpu.make_async_remote_copy(
                src_ref=edges.at[k], dst_ref=edges.at[2 + k], send_sem=edge_send.at[k],
                recv_sem=edge_recv.at[k], device_id={"rcv": to}, device_id_type=MESH,
            )
            for k, to in enumerate((left, right))
        ]

    def advance(step, more, ready):
        arrive(step)
        if more:
            for copy in first_copies(step + AHEAD):
                copy.start()
        if ready:
            finish(step - 1)
            work(step - 1)
        return 0

    advance(0, True, False)
    lax.fori_loop(1, 3, lambda step, _: advance(step, True, True), 0)
    edges[0] = out_ref[pad : 2 * pad, :]
    edges[1] = out_ref[rows : rows + pad, :]
    for copy in edge_copies():
        copy.start()
    lax.fori_loop(3, STEPS - AHEAD, lambda step, _: advance(step, True, True), 0)
    lax.fori_loop(STEPS - AHEAD, STEPS, lambda step, _: advance(step, False, True), 0)
    finish(STEPS - 1)
    work(STEPS - 1)

    for copy in edge_copies():
        copy.wait()
    zero = jnp.zeros((pad, samples), BF16)
    out_ref[0:pad, :] = jnp.where(line > 0, edges[3], zero)
    out_ref[rows + pad : rows + 2 * pad, :] = jnp.where(line < lines - 1, edges[2], zero)

    ends = [
        pltpu.make_async_copy(out_ref.at[part], out_hbm.at[part], out_sem.at[STEPS + k])
        for k, part in enumerate((pl.ds(0, pad), pl.ds(rows + pad, pad)))
    ]
    for copy in ends:
        copy.start()

    def sent(step, _):
        store(step).wait()
        for copy in first_copies(step) + (relays(step) if relay else []):
            copy.wait_send()
        return 0

    lax.fori_loop(0, STEPS, sent, 0)
    for copy in ends:
        copy.wait()


def local(record, slip_block, ghost_lag, order_ops):
    twins, lines = lax.axis_size("twin"), lax.axis_size("rcv")
    channels, rounds, samples = record.shape
    recs, orders = ghost_lag.shape
    groups, mine = channels // GROUP, recs * GROUP
    block = GROUP * rounds
    ways = max(twins, 4)
    far = pl.BlockSpec(memory_space=pl.ANY)
    padded = pl.pallas_call(
        functools.partial(clean_kernel, twins, lines),
        out_shape=jax.ShapeDtypeStruct(((channels + 4) * rounds, samples), BF16),
        in_specs=[far] * 4,
        out_specs=far,
        scratch_shapes=[
            pltpu.SMEM((recs,), jnp.int32),
            pltpu.SMEM((recs, orders), jnp.int32),
            pltpu.VMEM((channels * rounds, samples), BF16),
            pltpu.VMEM((orders * samples, samples), BF16),
            pltpu.VMEM(((channels + 4) * rounds, samples), BF16),
            pltpu.VMEM((groups, twins * mine, samples), BF16),
            pltpu.VMEM((twins, 8, 128), jnp.int32),
            pltpu.VMEM((orders * block, twins * mine), BF16),
            pltpu.VMEM((2 * block, orders * samples), BF16),
            pltpu.VMEM((4, 2 * rounds, samples), BF16),
            pltpu.SemaphoreType.DMA((3,)),
            pltpu.SemaphoreType.DMA((STEPS,)),
            pltpu.SemaphoreType.DMA((STEPS + 2,)),
            pltpu.SemaphoreType.DMA((twins,)),
            pltpu.SemaphoreType.DMA((twins,)),
            pltpu.SemaphoreType.DMA((STEPS, ways)),
            pltpu.SemaphoreType.DMA((STEPS, ways)),
            pltpu.SemaphoreType.DMA((2,)),
            pltpu.SemaphoreType.DMA((2,)),
        ],
        compiler_params=pltpu.CompilerParams(
            collective_id=0, has_side_effects=True, vmem_limit_bytes=60 * 2**20
        ),
        cost_estimate=pl.CostEstimate(
            flops=7 * 10**9, bytes_accessed=6 * 2**20, transcendentals=0
        ),
    )(
        slip_block, ghost_lag, record.reshape(channels * rounds, samples),
        order_ops.reshape(orders * samples, samples),
    )
    wide = padded.reshape(channels + 4, rounds, samples)
    before, middle, after = (wide[k : channels + k].astype(F32) for k in (1, 2, 3))
    return (0.5 * middle + 0.25 * (before + after)).astype(BF16)


def solution(mesh):
    placed = (P("rcv", None, "twin"), P("twin"), P("twin", None), P())
    return jax.shard_map(
        local, mesh=mesh, in_specs=placed, out_specs=P("rcv", None, "twin"), check_vma=False
    )
```

```python
import functools

import jax
import jax.numpy as jnp
from jax import lax
from jax.experimental import pallas as pl
from jax.experimental.pallas import tpu as pltpu
from jax.sharding import PartitionSpec as P

MESH = pl.DeviceIdType.MESH
GROUP = 16
STEPS = 8
AHEAD = 3
F32, BF16 = jnp.float32, jnp.bfloat16


def iota(shape, dim):
    return lax.broadcasted_iota(jnp.int32, shape, dim)


def clean_kernel(
    twins, lines, slip_hbm, lag_hbm, rec_hbm, ops_hbm, out_hbm,
    slip_ref, lag_ref, rec_ref, ops_ref, clean, out_ref,
    guides, lands, picks, spread, edges,
    small_sem, rec_sem, out_sem, land_send, land_recv, send_sem, recv_sem, edge_send, edge_recv,
):
    me = lax.axis_index("twin")
    line = lax.axis_index("rcv")
    recs, orders = lag_ref.shape
    rows, samples = rec_ref.shape
    groups, held, _ = guides.shape
    mine = held // twins
    rounds = rows // (groups * GROUP)
    block = GROUP * rounds
    per = groups // STEPS

    def chunk(step):
        return lax.rem(step * (STEPS - 1), STEPS)

    size = rows // STEPS

    def load(step):
        part = pl.ds(pl.multiple_of(chunk(step) * size, size), size)
        return pltpu.make_async_copy(rec_hbm.at[part], rec_ref.at[part], rec_sem.at[step])

    load_slip = pltpu.make_async_copy(slip_hbm, slip_ref, small_sem.at[0])
    load_lag = pltpu.make_async_copy(lag_hbm, lag_ref, small_sem.at[1])
    load_ops = pltpu.make_async_copy(ops_hbm, ops_ref, small_sem.at[2])
    load_slip.start()
    load_lag.start()
    for step in range(STEPS):
        load(step).start()
    load_ops.start()

    others = [lax.rem(me + d, twins) for d in range(1, twins)]
    left, right = lax.rem(line + lines - 1, lines), lax.rem(line + 1, lines)
    barrier = pltpu.get_barrier_semaphore()
    for other in others:
        pl.semaphore_signal(barrier, inc=1, device_id={"twin": other}, device_id_type=MESH)
    for other in (left, right):
        pl.semaphore_signal(barrier, inc=1, device_id={"rcv": other}, device_id_type=MESH)

    load_slip.wait()
    load_lag.wait()

    order_row, rec_lane = iota((8, 128), 0), (iota((8, 128), 1) // GROUP) % recs
    land = jnp.full((8, 128), -1, jnp.int32)
    for r in range(recs):
        for h in range(orders):
            here = (order_row == h) & (rec_lane == r)
            land = jnp.where(here, slip_ref[r] - lag_ref[r, h], land)
    lands[me] = land

    row, col = iota((mine, block), 0), iota((mine, block), 1)
    slip = jnp.zeros((mine, block), jnp.int32)
    for r in range(recs):
        slip = jnp.where(row // GROUP == r, slip_ref[r], slip)
    pick = (row % GROUP == col // rounds) & ((col % rounds) * twins + me == slip)
    pick = jnp.where(pick, 1.0, 0.0).astype(BF16)

    def own(twin):
        return pl.ds(pl.multiple_of(twin * mine, mine), mine)

    def move(step, begin, count, twin, to, index):
        part = guides.at[pl.ds(chunk(step) * per + begin, count), own(twin)]
        return pltpu.make_async_remote_copy(
            src_ref=part, dst_ref=part, send_sem=send_sem.at[step, index],
            recv_sem=recv_sem.at[step, index], device_id={"twin": to}, device_id_type=MESH,
        )

    def extract(step):
        load(step).wait()

        def one(i, _):
            g = chunk(step) * per + i
            rec = rec_ref[pl.ds(pl.multiple_of(g * block, block), block), :]
            guide = jnp.dot(pick, rec, preferred_element_type=F32)
            guides[g, own(me), :] = guide.astype(BF16)
            return 0
        lax.fori_loop(0, per, one, 0)

    relay = twins == 4
    if relay:
        across = (me // 2) * 2 + (1 - me % 2)
        along = (1 - me // 2) * 2 + me % 2
        half = per // 2

    def first_copies(step):
        if relay:
            return [move(step, 0, per, me, across, 0), move(step, 0, per, me, along, 1)]
        return [move(step, 0, per, me, other, d) for d, other in enumerate(others)]

    def relays(step):
        return [
            move(step, 0, half, along, across, 2),
            move(step, half, per - half, across, along, 3),
        ]

    extract(0)
    pl.semaphore_wait(barrier, twins + 1)
    for copy in first_copies(0):
        copy.start()

    def land_copy(d):
        return pltpu.make_async_remote_copy(
            src_ref=lands.at[me], dst_ref=lands.at[me], send_sem=land_send.at[d],
            recv_sem=land_recv.at[d], device_id={"twin": others[d]}, device_id_type=MESH,
        )

    for d in range(twins - 1):
        land_copy(d).start()

    def send_next(step, _):
        extract(step)
        for copy in first_copies(step):
            copy.start()
        return 0

    def extract_next(step, _):
        extract(step)
        return 0

    lax.fori_loop(1, AHEAD, send_next, 0)
    lax.fori_loop(AHEAD, STEPS, extract_next, 0)

    for d in range(twins - 1):
        land_copy(d).wait()

    row, col = iota((block, 128), 0), iota((block, 128), 1)
    same = row // rounds == col % GROUP
    goal = (row % rounds) * twins + me
    per_tile = 128 // mine
    for tile in range(held // 128):
        for h in range(orders):
            got = lands[tile * per_tile, h : h + 1, :]
            got = jnp.broadcast_to(got, (block, 128))
            for k in range(1, per_tile):
                more = lands[tile * per_tile + k, h : h + 1, :]
                got = jnp.where(col // mine == k, jnp.broadcast_to(more, (block, 128)), got)
            hit = jnp.where(same & (got == goal), 1.0, 0.0).astype(BF16)
            picks[h * block : (h + 1) * block, tile * 128 : (tile + 1) * 128] = hit
    load_ops.wait()

    pad = 2 * rounds

    def work(step):
        def one(i, _):
            for k in range(2):
                g = chunk(step) * per + i * 2 + k
                landed = jnp.dot(picks[...], guides[g], preferred_element_type=F32).astype(BF16)
                for h in range(orders):
                    spread[k * block : (k + 1) * block, h * samples : (h + 1) * samples] = landed[
                        h * block : (h + 1) * block
                    ]
            noise = jnp.dot(spread[...], ops_ref[...], preferred_element_type=F32)
            at = (chunk(step) * per + i * 2) * block
            at = pl.multiple_of(at, 2 * block)
            rec = rec_ref[pl.ds(at, 2 * block), :].astype(F32)
            clean[pl.ds(pl.multiple_of(at + pad, pad), 2 * block), :] = (rec - noise).astype(BF16)
            return 0
        lax.fori_loop(0, per // 2, one, 0)

    def store(begin, count, index):
        part = pl.ds(pl.multiple_of(begin * rounds, pad), count * rounds)
        return pltpu.make_async_copy(out_ref.at[part], out_hbm.at[part], out_sem.at[index])

    def smooth(begin, count, index):
        at = pl.multiple_of(begin * rounds, pad)
        wide = clean[pl.ds(at, (count + 4) * rounds), :].astype(F32)
        before, middle, after = (
            wide[k * rounds : (k + count) * rounds] for k in (1, 2, 3)
        )
        out_ref[pl.ds(at, count * rounds), :] = (
            0.5 * middle + 0.25 * (before + after)
        ).astype(BF16)
        store(begin, count, index).start()

    def arrive(step):
        if relay:
            for copy in first_copies(step):
                copy.wait_recv()
            for copy in relays(step):
                copy.start()

    def finish(step):
        for copy in relays(step) if relay else first_copies(step):
            copy.wait_recv()

    def edge_copies():
        return [
            pltpu.make_async_remote_copy(
                src_ref=edges.at[k], dst_ref=edges.at[2 + k], send_sem=edge_send.at[k],
                recv_sem=edge_recv.at[k], device_id={"rcv": to}, device_id_type=MESH,
            )
            for k, to in enumerate((left, right))
        ]

    chans = per * GROUP

    def window(step):
        return chunk(step) * chans + 2, chans, step

    def advance(step, more, ready, settled):
        arrive(step)
        if more:
            for copy in first_copies(step + AHEAD):
                copy.start()
        if ready:
            finish(step - 1)
            work(step - 1)
        if settled:
            smooth(*window(step - 1))
        return 0

    advance(0, True, False, False)
    lax.fori_loop(1, 3, lambda step, _: advance(step, True, True, False), 0)
    edges[0] = clean[pad : 2 * pad, :]
    edges[1] = clean[rows : rows + pad, :]
    for copy in edge_copies():
        copy.start()
    lax.fori_loop(3, STEPS - AHEAD, lambda step, _: advance(step, True, True, True), 0)
    lax.fori_loop(STEPS - AHEAD, STEPS, lambda step, _: advance(step, False, True, True), 0)

    for copy in edge_copies():
        copy.wait()
    zero = jnp.zeros((pad, samples), BF16)
    clean[0:pad, :] = jnp.where(line > 0, edges[3], zero)
    clean[rows + pad : rows + 2 * pad, :] = jnp.where(line < lines - 1, edges[2], zero)
    last = [
        (0, chans - 2, 0),
        ((STEPS - 1) * chans + 2, chans - 2, 1),
        (chans - 2, chans + 4, STEPS - 1),
    ]
    smooth(*last[0])
    smooth(*last[1])
    finish(STEPS - 1)
    work(STEPS - 1)
    smooth(*last[2])

    def sent(step, _):
        for copy in first_copies(step) + (relays(step) if relay else []):
            copy.wait_send()
        return 0

    lax.fori_loop(0, STEPS, sent, 0)

    def stored(step, _):
        store(*window(step)).wait()
        return 0

    lax.fori_loop(2, STEPS - 1, stored, 0)
    for piece in last:
        store(*piece).wait()


def local(record, slip_block, ghost_lag, order_ops):
    twins, lines = lax.axis_size("twin"), lax.axis_size("rcv")
    channels, rounds, samples = record.shape
    recs, orders = ghost_lag.shape
    groups, mine = channels // GROUP, recs * GROUP
    block = GROUP * rounds
    ways = max(twins, 4)
    far = pl.BlockSpec(memory_space=pl.ANY)
    smoothed = pl.pallas_call(
        functools.partial(clean_kernel, twins, lines),
        out_shape=jax.ShapeDtypeStruct((channels * rounds, samples), BF16),
        in_specs=[far] * 4,
        out_specs=far,
        scratch_shapes=[
            pltpu.SMEM((recs,), jnp.int32),
            pltpu.SMEM((recs, orders), jnp.int32),
            pltpu.VMEM((channels * rounds, samples), BF16),
            pltpu.VMEM((orders * samples, samples), BF16),
            pltpu.VMEM(((channels + 4) * rounds, samples), BF16),
            pltpu.VMEM((channels * rounds, samples), BF16),
            pltpu.VMEM((groups, twins * mine, samples), BF16),
            pltpu.VMEM((twins, 8, 128), jnp.int32),
            pltpu.VMEM((orders * block, twins * mine), BF16),
            pltpu.VMEM((2 * block, orders * samples), BF16),
            pltpu.VMEM((4, 2 * rounds, samples), BF16),
            pltpu.SemaphoreType.DMA((3,)),
            pltpu.SemaphoreType.DMA((STEPS,)),
            pltpu.SemaphoreType.DMA((STEPS,)),
            pltpu.SemaphoreType.DMA((twins,)),
            pltpu.SemaphoreType.DMA((twins,)),
            pltpu.SemaphoreType.DMA((STEPS, ways)),
            pltpu.SemaphoreType.DMA((STEPS, ways)),
            pltpu.SemaphoreType.DMA((2,)),
            pltpu.SemaphoreType.DMA((2,)),
        ],
        compiler_params=pltpu.CompilerParams(
            collective_id=0, has_side_effects=True, vmem_limit_bytes=60 * 2**20
        ),
        cost_estimate=pl.CostEstimate(
            flops=7 * 10**9, bytes_accessed=6 * 2**20, transcendentals=0
        ),
    )(
        slip_block, ghost_lag, record.reshape(channels * rounds, samples),
        order_ops.reshape(orders * samples, samples),
    )
    return smoothed.reshape(channels, rounds, samples)


def solution(mesh):
    placed = (P("rcv", None, "twin"), P("twin"), P("twin", None), P())
    return jax.shard_map(
        local, mesh=mesh, in_specs=placed, out_specs=P("rcv", None, "twin"), check_vma=False
    )
```

```python
import functools

import jax
import jax.numpy as jnp
from jax import lax
from jax.experimental import pallas as pl
from jax.experimental.pallas import tpu as pltpu
from jax.sharding import PartitionSpec as P

MESH = pl.DeviceIdType.MESH
GROUP = 16
STEPS = 8
AHEAD = 3
F32, BF16 = jnp.float32, jnp.bfloat16


def iota(shape, dim):
    return lax.broadcasted_iota(jnp.int32, shape, dim)


def clean_kernel(
    twins, lines, slip_hbm, lag_hbm, rec_hbm, ops_hbm, out_ref,
    slip_ref, lag_ref, rec_ref, ops_ref, clean,
    guides, lands, picks, spread, edges,
    small_sem, rec_sem, land_send, land_recv, send_sem, recv_sem, edge_send, edge_recv,
):
    me = lax.axis_index("twin")
    line = lax.axis_index("rcv")
    recs, orders = lag_ref.shape
    rows, samples = rec_ref.shape
    groups, held, _ = guides.shape
    mine = held // twins
    rounds = rows // (groups * GROUP)
    block = GROUP * rounds
    per = groups // STEPS

    def chunk(step):
        return lax.rem(step * (STEPS - 1), STEPS)

    size = rows // STEPS

    def load(step):
        part = pl.ds(pl.multiple_of(chunk(step) * size, size), size)
        return pltpu.make_async_copy(rec_hbm.at[part], rec_ref.at[part], rec_sem.at[step])

    load_slip = pltpu.make_async_copy(slip_hbm, slip_ref, small_sem.at[0])
    load_lag = pltpu.make_async_copy(lag_hbm, lag_ref, small_sem.at[1])
    load_ops = pltpu.make_async_copy(ops_hbm, ops_ref, small_sem.at[2])
    load_slip.start()
    load_lag.start()
    for step in range(STEPS):
        load(step).start()
    load_ops.start()

    others = [lax.rem(me + d, twins) for d in range(1, twins)]
    left, right = lax.rem(line + lines - 1, lines), lax.rem(line + 1, lines)
    barrier = pltpu.get_barrier_semaphore()
    for other in others:
        pl.semaphore_signal(barrier, inc=1, device_id={"twin": other}, device_id_type=MESH)
    for other in (left, right):
        pl.semaphore_signal(barrier, inc=1, device_id={"rcv": other}, device_id_type=MESH)

    load_slip.wait()
    load_lag.wait()

    order_row, rec_lane = iota((8, 128), 0), (iota((8, 128), 1) // GROUP) % recs
    land = jnp.full((8, 128), -1, jnp.int32)
    for r in range(recs):
        for h in range(orders):
            here = (order_row == h) & (rec_lane == r)
            land = jnp.where(here, slip_ref[r] - lag_ref[r, h], land)
    lands[me] = land

    row, col = iota((mine, block), 0), iota((mine, block), 1)
    slip = jnp.zeros((mine, block), jnp.int32)
    for r in range(recs):
        slip = jnp.where(row // GROUP == r, slip_ref[r], slip)
    pick = (row % GROUP == col // rounds) & ((col % rounds) * twins + me == slip)
    pick = jnp.where(pick, 1.0, 0.0).astype(BF16)

    def own(twin):
        return pl.ds(pl.multiple_of(twin * mine, mine), mine)

    def move(step, begin, count, twin, to, index):
        part = guides.at[pl.ds(chunk(step) * per + begin, count), own(twin)]
        return pltpu.make_async_remote_copy(
            src_ref=part, dst_ref=part, send_sem=send_sem.at[step, index],
            recv_sem=recv_sem.at[step, index], device_id={"twin": to}, device_id_type=MESH,
        )

    def extract(step):
        load(step).wait()

        def one(i, _):
            g = chunk(step) * per + i
            rec = rec_ref[pl.ds(pl.multiple_of(g * block, block), block), :]
            guide = jnp.dot(pick, rec, preferred_element_type=F32)
            guides[g, own(me), :] = guide.astype(BF16)
            return 0
        lax.fori_loop(0, per, one, 0)

    relay = twins == 4
    if relay:
        across = (me // 2) * 2 + (1 - me % 2)
        along = (1 - me // 2) * 2 + me % 2
        half = per // 2

    def first_copies(step):
        if relay:
            return [move(step, 0, per, me, across, 0), move(step, 0, per, me, along, 1)]
        return [move(step, 0, per, me, other, d) for d, other in enumerate(others)]

    def relays(step):
        return [
            move(step, 0, half, along, across, 2),
            move(step, half, per - half, across, along, 3),
        ]

    extract(0)
    pl.semaphore_wait(barrier, twins + 1)
    for copy in first_copies(0):
        copy.start()

    def land_copy(d):
        return pltpu.make_async_remote_copy(
            src_ref=lands.at[me], dst_ref=lands.at[me], send_sem=land_send.at[d],
            recv_sem=land_recv.at[d], device_id={"twin": others[d]}, device_id_type=MESH,
        )

    for d in range(twins - 1):
        land_copy(d).start()

    def send_next(step, _):
        extract(step)
        for copy in first_copies(step):
            copy.start()
        return 0

    def extract_next(step, _):
        extract(step)
        return 0

    lax.fori_loop(1, AHEAD, send_next, 0)
    lax.fori_loop(AHEAD, STEPS, extract_next, 0)

    for d in range(twins - 1):
        land_copy(d).wait()

    row, col = iota((block, 128), 0), iota((block, 128), 1)
    same = row // rounds == col % GROUP
    goal = (row % rounds) * twins + me
    per_tile = 128 // mine
    for tile in range(held // 128):
        for h in range(orders):
            got = lands[tile * per_tile, h : h + 1, :]
            got = jnp.broadcast_to(got, (block, 128))
            for k in range(1, per_tile):
                more = lands[tile * per_tile + k, h : h + 1, :]
                got = jnp.where(col // mine == k, jnp.broadcast_to(more, (block, 128)), got)
            hit = jnp.where(same & (got == goal), 1.0, 0.0).astype(BF16)
            picks[h * block : (h + 1) * block, tile * 128 : (tile + 1) * 128] = hit
    load_ops.wait()

    pad = 2 * rounds

    def work(step):
        def one(i, _):
            for k in range(2):
                g = chunk(step) * per + i * 2 + k
                landed = jnp.dot(picks[...], guides[g], preferred_element_type=F32).astype(BF16)
                for h in range(orders):
                    spread[k * block : (k + 1) * block, h * samples : (h + 1) * samples] = landed[
                        h * block : (h + 1) * block
                    ]
            noise = jnp.dot(spread[...], ops_ref[...], preferred_element_type=F32)
            at = (chunk(step) * per + i * 2) * block
            at = pl.multiple_of(at, 2 * block)
            rec = rec_ref[pl.ds(at, 2 * block), :].astype(F32)
            clean[pl.ds(pl.multiple_of(at + pad, pad), 2 * block), :] = (rec - noise).astype(BF16)
            return 0
        lax.fori_loop(0, per // 2, one, 0)

    def smooth(begin, count):
        at = pl.multiple_of(begin * rounds, pad)
        wide = clean[pl.ds(at, (count + 4) * rounds), :].astype(F32)
        before, middle, after = (
            wide[k * rounds : (k + count) * rounds] for k in (1, 2, 3)
        )
        out_ref[pl.ds(at, count * rounds), :] = (
            0.5 * middle + 0.25 * (before + after)
        ).astype(BF16)

    def arrive(step):
        if relay:
            for copy in first_copies(step):
                copy.wait_recv()
            for copy in relays(step):
                copy.start()

    def finish(step):
        for copy in relays(step) if relay else first_copies(step):
            copy.wait_recv()

    def edge_copies():
        return [
            pltpu.make_async_remote_copy(
                src_ref=edges.at[k], dst_ref=edges.at[2 + k], send_sem=edge_send.at[k],
                recv_sem=edge_recv.at[k], device_id={"rcv": to}, device_id_type=MESH,
            )
            for k, to in enumerate((left, right))
        ]

    chans = per * GROUP

    def window(step):
        return chunk(step) * chans + 2, chans

    def advance(step, more, ready, settled):
        arrive(step)
        if more:
            for copy in first_copies(step + AHEAD):
                copy.start()
        if ready:
            finish(step - 1)
            work(step - 1)
        if settled:
            smooth(*window(step - 1))
        return 0

    advance(0, True, False, False)
    lax.fori_loop(1, 3, lambda step, _: advance(step, True, True, False), 0)
    edges[0] = clean[pad : 2 * pad, :]
    edges[1] = clean[rows : rows + pad, :]
    for copy in edge_copies():
        copy.start()
    lax.fori_loop(3, STEPS - AHEAD, lambda step, _: advance(step, True, True, True), 0)
    lax.fori_loop(STEPS - AHEAD, STEPS, lambda step, _: advance(step, False, True, True), 0)

    for copy in edge_copies():
        copy.wait()
    zero = jnp.zeros((pad, samples), BF16)
    clean[0:pad, :] = jnp.where(line > 0, edges[3], zero)
    clean[rows + pad : rows + 2 * pad, :] = jnp.where(line < lines - 1, edges[2], zero)
    smooth(0, chans - 2)
    smooth((STEPS - 1) * chans + 2, chans - 2)
    finish(STEPS - 1)
    work(STEPS - 1)
    smooth(chans - 2, chans + 4)

    def sent(step, _):
        for copy in first_copies(step) + (relays(step) if relay else []):
            copy.wait_send()
        return 0

    lax.fori_loop(0, STEPS, sent, 0)


def local(record, slip_block, ghost_lag, order_ops):
    twins, lines = lax.axis_size("twin"), lax.axis_size("rcv")
    channels, rounds, samples = record.shape
    recs, orders = ghost_lag.shape
    groups, mine = channels // GROUP, recs * GROUP
    block = GROUP * rounds
    ways = max(twins, 4)
    far = pl.BlockSpec(memory_space=pltpu.HBM)
    smoothed = pl.pallas_call(
        functools.partial(clean_kernel, twins, lines),
        out_shape=pltpu.VMEM((channels * rounds, samples), BF16),
        in_specs=[far] * 4,
        out_specs=pl.BlockSpec(memory_space=pltpu.VMEM),
        scratch_shapes=[
            pltpu.SMEM((recs,), jnp.int32),
            pltpu.SMEM((recs, orders), jnp.int32),
            pltpu.VMEM((channels * rounds, samples), BF16),
            pltpu.VMEM((orders * samples, samples), BF16),
            pltpu.VMEM(((channels + 4) * rounds, samples), BF16),
            pltpu.VMEM((groups, twins * mine, samples), BF16),
            pltpu.VMEM((twins, 8, 128), jnp.int32),
            pltpu.VMEM((orders * block, twins * mine), BF16),
            pltpu.VMEM((2 * block, orders * samples), BF16),
            pltpu.VMEM((4, 2 * rounds, samples), BF16),
            pltpu.SemaphoreType.DMA((3,)),
            pltpu.SemaphoreType.DMA((STEPS,)),
            pltpu.SemaphoreType.DMA((twins,)),
            pltpu.SemaphoreType.DMA((twins,)),
            pltpu.SemaphoreType.DMA((STEPS, ways)),
            pltpu.SemaphoreType.DMA((STEPS, ways)),
            pltpu.SemaphoreType.DMA((2,)),
            pltpu.SemaphoreType.DMA((2,)),
        ],
        compiler_params=pltpu.CompilerParams(
            collective_id=0, has_side_effects=True, vmem_limit_bytes=56 * 2**20
        ),
        cost_estimate=pl.CostEstimate(
            flops=7 * 10**9, bytes_accessed=6 * 2**20, transcendentals=0
        ),
    )(
        slip_block, ghost_lag, record.reshape(channels * rounds, samples),
        order_ops.reshape(orders * samples, samples),
    )
    return smoothed.reshape(channels, rounds, samples)


def solution(mesh):
    placed = (P("rcv", None, "twin"), P("twin"), P("twin", None), P())
    return jax.shard_map(
        local, mesh=mesh, in_specs=placed, out_specs=P("rcv", None, "twin"), check_vma=False
    )
```

```python
import functools

import jax
import jax.numpy as jnp
from jax import lax
from jax.experimental import pallas as pl
from jax.experimental.pallas import tpu as pltpu
from jax.sharding import PartitionSpec as P

MESH = pl.DeviceIdType.MESH
GROUP = 16
STEPS = 16
AHEAD = 5
F32, BF16 = jnp.float32, jnp.bfloat16


def iota(shape, dim):
    return lax.broadcasted_iota(jnp.int32, shape, dim)


def clean_kernel(
    twins, lines, slip_hbm, lag_hbm, rec_hbm, ops_hbm, out_ref,
    slip_ref, lag_ref, rec_ref, ops_ref, clean,
    guides, lands, picks, spread, edges,
    small_sem, rec_sem, land_send, land_recv, send_sem, recv_sem, edge_send, edge_recv,
):
    me = lax.axis_index("twin")
    line = lax.axis_index("rcv")
    recs, orders = lag_ref.shape
    rows, samples = rec_ref.shape
    groups, held, _ = guides.shape
    mine = held // twins
    rounds = rows // (groups * GROUP)
    block = GROUP * rounds
    per = groups // STEPS

    def chunk(step):
        return lax.rem(step * (STEPS - 1), STEPS)

    size = rows // STEPS

    def load(step):
        part = pl.ds(pl.multiple_of(chunk(step) * size, size), size)
        return pltpu.make_async_copy(rec_hbm.at[part], rec_ref.at[part], rec_sem.at[step])

    load_slip = pltpu.make_async_copy(slip_hbm, slip_ref, small_sem.at[0])
    load_lag = pltpu.make_async_copy(lag_hbm, lag_ref, small_sem.at[1])
    load_ops = pltpu.make_async_copy(ops_hbm, ops_ref, small_sem.at[2])
    load_slip.start()
    load_lag.start()
    for step in range(STEPS):
        load(step).start()
    load_ops.start()

    others = [lax.rem(me + d, twins) for d in range(1, twins)]
    left, right = lax.rem(line + lines - 1, lines), lax.rem(line + 1, lines)
    barrier = pltpu.get_barrier_semaphore()
    for other in others:
        pl.semaphore_signal(barrier, inc=1, device_id={"twin": other}, device_id_type=MESH)
    for other in (left, right):
        pl.semaphore_signal(barrier, inc=1, device_id={"rcv": other}, device_id_type=MESH)

    load_slip.wait()
    load_lag.wait()

    order_row, rec_lane = iota((8, 128), 0), (iota((8, 128), 1) // GROUP) % recs
    land = jnp.full((8, 128), -1, jnp.int32)
    for r in range(recs):
        for h in range(orders):
            here = (order_row == h) & (rec_lane == r)
            land = jnp.where(here, slip_ref[r] - lag_ref[r, h], land)
    lands[me] = land

    row, col = iota((mine, block), 0), iota((mine, block), 1)
    slip = jnp.zeros((mine, block), jnp.int32)
    for r in range(recs):
        slip = jnp.where(row // GROUP == r, slip_ref[r], slip)
    pick = (row % GROUP == col // rounds) & ((col % rounds) * twins + me == slip)
    pick = jnp.where(pick, 1.0, 0.0).astype(BF16)

    half = mine // 2

    def own(twin, begin=0, count=mine):
        return pl.ds(pl.multiple_of(twin * mine + begin, half), count)

    def move(step, begin, count, twin, to, index):
        part = guides.at[pl.ds(chunk(step) * per, per), own(twin, begin, count)]
        return pltpu.make_async_remote_copy(
            src_ref=part, dst_ref=part, send_sem=send_sem.at[step, index],
            recv_sem=recv_sem.at[step, index], device_id={"twin": to}, device_id_type=MESH,
        )

    def extract(step):
        load(step).wait()

        def one(i, _):
            g = chunk(step) * per + i
            rec = rec_ref[pl.ds(pl.multiple_of(g * block, block), block), :]
            guide = jnp.dot(pick, rec, preferred_element_type=F32)
            guides[g, own(me), :] = guide.astype(BF16)
            return 0
        lax.fori_loop(0, per, one, 0)

    relay = twins == 4
    if relay:
        across = (me // 2) * 2 + (1 - me % 2)
        along = (1 - me // 2) * 2 + me % 2

    def first_copies(step):
        if relay:
            return [move(step, 0, mine, me, across, 0), move(step, 0, mine, me, along, 1)]
        return [move(step, 0, mine, me, other, d) for d, other in enumerate(others)]

    def relays(step):
        return [
            move(step, 0, half, along, across, 2),
            move(step, half, half, across, along, 3),
        ]

    extract(0)
    pl.semaphore_wait(barrier, twins + 1)
    for copy in first_copies(0):
        copy.start()

    def land_copy(d):
        return pltpu.make_async_remote_copy(
            src_ref=lands.at[me], dst_ref=lands.at[me], send_sem=land_send.at[d],
            recv_sem=land_recv.at[d], device_id={"twin": others[d]}, device_id_type=MESH,
        )

    for d in range(twins - 1):
        land_copy(d).start()

    def send_next(step, _):
        extract(step)
        for copy in first_copies(step):
            copy.start()
        return 0

    def extract_next(step, _):
        extract(step)
        return 0

    lax.fori_loop(1, AHEAD, send_next, 0)
    lax.fori_loop(AHEAD, STEPS, extract_next, 0)

    for d in range(twins - 1):
        land_copy(d).wait()

    row, col = iota((block, 128), 0), iota((block, 128), 1)
    same = row // rounds == col % GROUP
    goal = (row % rounds) * twins + me
    per_tile = 128 // mine
    for tile in range(held // 128):
        for h in range(orders):
            got = lands[tile * per_tile, h : h + 1, :]
            got = jnp.broadcast_to(got, (block, 128))
            for k in range(1, per_tile):
                more = lands[tile * per_tile + k, h : h + 1, :]
                got = jnp.where(col // mine == k, jnp.broadcast_to(more, (block, 128)), got)
            hit = jnp.where(same & (got == goal), 1.0, 0.0).astype(BF16)
            picks[h * block : (h + 1) * block, tile * 128 : (tile + 1) * 128] = hit
    load_ops.wait()

    pad = 2 * rounds

    def work(step):
        for k in range(per):
            g = chunk(step) * per + k
            landed = jnp.dot(picks[...], guides[g], preferred_element_type=F32).astype(BF16)
            for h in range(orders):
                spread[k * block : (k + 1) * block, h * samples : (h + 1) * samples] = landed[
                    h * block : (h + 1) * block
                ]
        noise = jnp.dot(spread[...], ops_ref[...], preferred_element_type=F32)
        at = pl.multiple_of(chunk(step) * size, size)
        rec = rec_ref[pl.ds(at, size), :].astype(F32)
        clean[pl.ds(pl.multiple_of(at + pad, pad), size), :] = (rec - noise).astype(BF16)

    def smooth(begin, count):
        at = pl.multiple_of(begin * rounds, pad)
        wide = clean[pl.ds(at, (count + 4) * rounds), :].astype(F32)
        before, middle, after = (
            wide[k * rounds : (k + count) * rounds] for k in (1, 2, 3)
        )
        out_ref[pl.ds(at, count * rounds), :] = (
            0.5 * middle + 0.25 * (before + after)
        ).astype(BF16)

    def arrive(step):
        if relay:
            for copy in first_copies(step):
                copy.wait_recv()
            for copy in relays(step):
                copy.start()

    def finish(step):
        for copy in relays(step) if relay else first_copies(step):
            copy.wait_recv()

    def edge_copies():
        return [
            pltpu.make_async_remote_copy(
                src_ref=edges.at[k], dst_ref=edges.at[2 + k], send_sem=edge_send.at[k],
                recv_sem=edge_recv.at[k], device_id={"rcv": to}, device_id_type=MESH,
            )
            for k, to in enumerate((left, right))
        ]

    chans = per * GROUP

    def window(step):
        return chunk(step) * chans + 2, chans

    def advance(step, more, ready, settled):
        arrive(step)
        if more:
            for copy in first_copies(step + AHEAD):
                copy.start()
        if ready:
            finish(step - 1)
            work(step - 1)
        if settled:
            smooth(*window(step - 1))
        return 0

    advance(0, True, False, False)
    lax.fori_loop(1, 3, lambda step, _: advance(step, True, True, False), 0)
    edges[0] = clean[pad : 2 * pad, :]
    edges[1] = clean[rows : rows + pad, :]
    for copy in edge_copies():
        copy.start()
    lax.fori_loop(3, STEPS - AHEAD, lambda step, _: advance(step, True, True, True), 0)
    lax.fori_loop(STEPS - AHEAD, STEPS, lambda step, _: advance(step, False, True, True), 0)

    for copy in edge_copies():
        copy.wait()
    zero = jnp.zeros((pad, samples), BF16)
    clean[0:pad, :] = jnp.where(line > 0, edges[3], zero)
    clean[rows + pad : rows + 2 * pad, :] = jnp.where(line < lines - 1, edges[2], zero)
    smooth(0, chans - 2)
    smooth((STEPS - 1) * chans + 2, chans - 2)
    finish(STEPS - 1)
    work(STEPS - 1)
    smooth(chans - 2, chans + 4)

    def sent(step, _):
        for copy in first_copies(step) + (relays(step) if relay else []):
            copy.wait_send()
        return 0

    lax.fori_loop(0, STEPS, sent, 0)


def local(record, slip_block, ghost_lag, order_ops):
    twins, lines = lax.axis_size("twin"), lax.axis_size("rcv")
    channels, rounds, samples = record.shape
    recs, orders = ghost_lag.shape
    groups, mine = channels // GROUP, recs * GROUP
    block = GROUP * rounds
    ways = max(twins, 4)
    far = pl.BlockSpec(memory_space=pltpu.HBM)
    smoothed = pl.pallas_call(
        functools.partial(clean_kernel, twins, lines),
        out_shape=pltpu.VMEM((channels * rounds, samples), BF16),
        in_specs=[far] * 4,
        out_specs=pl.BlockSpec(memory_space=pltpu.VMEM),
        scratch_shapes=[
            pltpu.SMEM((recs,), jnp.int32),
            pltpu.SMEM((recs, orders), jnp.int32),
            pltpu.VMEM((channels * rounds, samples), BF16),
            pltpu.VMEM((orders * samples, samples), BF16),
            pltpu.VMEM(((channels + 4) * rounds, samples), BF16),
            pltpu.VMEM((groups, twins * mine, samples), BF16),
            pltpu.VMEM((twins, 8, 128), jnp.int32),
            pltpu.VMEM((orders * block, twins * mine), BF16),
            pltpu.VMEM((channels * rounds // STEPS, orders * samples), BF16),
            pltpu.VMEM((4, 2 * rounds, samples), BF16),
            pltpu.SemaphoreType.DMA((3,)),
            pltpu.SemaphoreType.DMA((STEPS,)),
            pltpu.SemaphoreType.DMA((twins,)),
            pltpu.SemaphoreType.DMA((twins,)),
            pltpu.SemaphoreType.DMA((STEPS, ways)),
            pltpu.SemaphoreType.DMA((STEPS, ways)),
            pltpu.SemaphoreType.DMA((2,)),
            pltpu.SemaphoreType.DMA((2,)),
        ],
        compiler_params=pltpu.CompilerParams(
            collective_id=0, has_side_effects=True, vmem_limit_bytes=56 * 2**20
        ),
        cost_estimate=pl.CostEstimate(
            flops=7 * 10**9, bytes_accessed=6 * 2**20, transcendentals=0
        ),
    )(
        slip_block, ghost_lag, record.reshape(channels * rounds, samples),
        order_ops.reshape(orders * samples, samples),
    )
    return smoothed.reshape(channels, rounds, samples)


def solution(mesh):
    placed = (P("rcv", None, "twin"), P("twin"), P("twin", None), P())
    return jax.shard_map(
        local, mesh=mesh, in_specs=placed, out_specs=P("rcv", None, "twin"), check_vma=False
    )
```

```python
import functools

import jax
import jax.numpy as jnp
from jax import lax
from jax.experimental import pallas as pl
from jax.experimental.pallas import tpu as pltpu
from jax.sharding import PartitionSpec as P

MESH = pl.DeviceIdType.MESH
GROUP = 16
STEPS = 8
AHEAD = 2
F32, BF16 = jnp.float32, jnp.bfloat16


def iota(shape, dim):
    return lax.broadcasted_iota(jnp.int32, shape, dim)


def clean_kernel(
    twins, lines, slip_hbm, lag_hbm, rec_hbm, ops_hbm, out_ref,
    slip_ref, lag_ref, rec_ref, ops_ref, clean,
    guides, lands, picks, spread, edges,
    small_sem, rec_sem, land_send, land_recv, send_sem, recv_sem, edge_send, edge_recv,
):
    me = lax.axis_index("twin")
    line = lax.axis_index("rcv")
    recs, orders = lag_ref.shape
    rows, samples = rec_ref.shape
    groups, held, _ = guides.shape
    mine = held // twins
    rounds = rows // (groups * GROUP)
    block = GROUP * rounds
    per = groups // STEPS

    def chunk(step):
        return lax.rem(step * (STEPS - 1), STEPS)

    size = rows // STEPS

    def load(step):
        part = pl.ds(pl.multiple_of(chunk(step) * size, size), size)
        return pltpu.make_async_copy(rec_hbm.at[part], rec_ref.at[part], rec_sem.at[step])

    load_slip = pltpu.make_async_copy(slip_hbm, slip_ref, small_sem.at[0])
    load_lag = pltpu.make_async_copy(lag_hbm, lag_ref, small_sem.at[1])
    load_ops = pltpu.make_async_copy(ops_hbm, ops_ref, small_sem.at[2])
    load_slip.start()
    load_lag.start()
    for step in range(STEPS):
        load(step).start()
    load_ops.start()

    others = [lax.rem(me + d, twins) for d in range(1, twins)]
    left, right = lax.rem(line + lines - 1, lines), lax.rem(line + 1, lines)
    barrier = pltpu.get_barrier_semaphore()
    for other in others:
        pl.semaphore_signal(barrier, inc=1, device_id={"twin": other}, device_id_type=MESH)
    for other in (left, right):
        pl.semaphore_signal(barrier, inc=1, device_id={"rcv": other}, device_id_type=MESH)

    load_slip.wait()
    load_lag.wait()

    order_row, rec_lane = iota((8, 128), 0), (iota((8, 128), 1) // GROUP) % recs
    land = jnp.full((8, 128), -1, jnp.int32)
    for r in range(recs):
        for h in range(orders):
            here = (order_row == h) & (rec_lane == r)
            land = jnp.where(here, slip_ref[r] - lag_ref[r, h], land)
    lands[me] = land

    row, col = iota((mine, block), 0), iota((mine, block), 1)
    slip = jnp.zeros((mine, block), jnp.int32)
    for r in range(recs):
        slip = jnp.where(row // GROUP == r, slip_ref[r], slip)
    pick = (row % GROUP == col // rounds) & ((col % rounds) * twins + me == slip)
    pick = jnp.where(pick, 1.0, 0.0).astype(BF16)

    def own(twin):
        return pl.ds(pl.multiple_of(twin * mine, mine), mine)

    def move(step, begin, count, twin, to, index):
        part = guides.at[pl.ds(chunk(step) * per + begin, count), own(twin)]
        return pltpu.make_async_remote_copy(
            src_ref=part, dst_ref=part, send_sem=send_sem.at[step, index],
            recv_sem=recv_sem.at[step, index], device_id={"twin": to}, device_id_type=MESH,
        )

    def extract(step):
        load(step).wait()

        def one(i, _):
            g = chunk(step) * per + i
            rec = rec_ref[pl.ds(pl.multiple_of(g * block, block), block), :]
            guide = jnp.dot(pick, rec, preferred_element_type=F32)
            guides[g, own(me), :] = guide.astype(BF16)
            return 0
        lax.fori_loop(0, per, one, 0)

    relay = twins == 4
    if relay:
        across = (me // 2) * 2 + (1 - me % 2)
        along = (1 - me // 2) * 2 + me % 2
        half = per // 2

    def first_copies(step):
        if relay:
            return [move(step, 0, per, me, across, 0), move(step, 0, per, me, along, 1)]
        return [move(step, 0, per, me, other, d) for d, other in enumerate(others)]

    def relays(step):
        return [
            move(step, 0, half, along, across, 2),
            move(step, half, per - half, across, along, 3),
        ]

    extract(0)
    pl.semaphore_wait(barrier, twins + 1)
    for copy in first_copies(0):
        copy.start()

    def land_copy(d):
        return pltpu.make_async_remote_copy(
            src_ref=lands.at[me], dst_ref=lands.at[me], send_sem=land_send.at[d],
            recv_sem=land_recv.at[d], device_id={"twin": others[d]}, device_id_type=MESH,
        )

    for d in range(twins - 1):
        land_copy(d).start()

    def send_next(step, _):
        extract(step)
        for copy in first_copies(step):
            copy.start()
        return 0

    def extract_next(step, _):
        extract(step)
        return 0

    lax.fori_loop(1, AHEAD, send_next, 0)
    lax.fori_loop(AHEAD, STEPS, extract_next, 0)

    for d in range(twins - 1):
        land_copy(d).wait()

    row, col = iota((block, 128), 0), iota((block, 128), 1)
    same = row // rounds == col % GROUP
    goal = (row % rounds) * twins + me
    per_tile = 128 // mine
    for tile in range(held // 128):
        for h in range(orders):
            got = lands[tile * per_tile, h : h + 1, :]
            got = jnp.broadcast_to(got, (block, 128))
            for k in range(1, per_tile):
                more = lands[tile * per_tile + k, h : h + 1, :]
                got = jnp.where(col // mine == k, jnp.broadcast_to(more, (block, 128)), got)
            hit = jnp.where(same & (got == goal), 1.0, 0.0).astype(BF16)
            picks[h * block : (h + 1) * block, tile * 128 : (tile + 1) * 128] = hit
    load_ops.wait()

    pad = 2 * rounds

    def work(step):
        def one(i, _):
            for k in range(2):
                g = chunk(step) * per + i * 2 + k
                landed = jnp.dot(picks[...], guides[g], preferred_element_type=F32).astype(BF16)
                for h in range(orders):
                    spread[k * block : (k + 1) * block, h * samples : (h + 1) * samples] = landed[
                        h * block : (h + 1) * block
                    ]
            noise = jnp.dot(spread[...], ops_ref[...], preferred_element_type=F32)
            at = (chunk(step) * per + i * 2) * block
            at = pl.multiple_of(at, 2 * block)
            rec = rec_ref[pl.ds(at, 2 * block), :].astype(F32)
            clean[pl.ds(pl.multiple_of(at + pad, pad), 2 * block), :] = (rec - noise).astype(BF16)
            return 0
        lax.fori_loop(0, per // 2, one, 0)

    def smooth(begin, count):
        at = pl.multiple_of(begin * rounds, pad)
        wide = clean[pl.ds(at, (count + 4) * rounds), :].astype(F32)
        before, middle, after = (
            wide[k * rounds : (k + count) * rounds] for k in (1, 2, 3)
        )
        out_ref[pl.ds(at, count * rounds), :] = (
            0.5 * middle + 0.25 * (before + after)
        ).astype(BF16)

    def arrive(step):
        if relay:
            for copy in first_copies(step):
                copy.wait_recv()
            for copy in relays(step):
                copy.start()

    def finish(step):
        for copy in relays(step) if relay else first_copies(step):
            copy.wait_recv()

    def edge_copies():
        return [
            pltpu.make_async_remote_copy(
                src_ref=edges.at[k], dst_ref=edges.at[2 + k], send_sem=edge_send.at[k],
                recv_sem=edge_recv.at[k], device_id={"rcv": to}, device_id_type=MESH,
            )
            for k, to in enumerate((left, right))
        ]

    chans = per * GROUP

    def window(step):
        return chunk(step) * chans + 2, chans

    def advance(step, more, ready, settled):
        arrive(step)
        if more:
            for copy in first_copies(step + AHEAD):
                copy.start()
        if ready:
            finish(step - 1)
            work(step - 1)
        if settled:
            smooth(*window(step - 1))
        return 0

    advance(0, True, False, False)
    lax.fori_loop(1, 3, lambda step, _: advance(step, True, True, False), 0)
    edges[0] = clean[pad : 2 * pad, :]
    edges[1] = clean[rows : rows + pad, :]
    for copy in edge_copies():
        copy.start()
    lax.fori_loop(3, STEPS - AHEAD, lambda step, _: advance(step, True, True, True), 0)
    lax.fori_loop(STEPS - AHEAD, STEPS, lambda step, _: advance(step, False, True, True), 0)

    for copy in edge_copies():
        copy.wait()
    zero = jnp.zeros((pad, samples), BF16)
    clean[0:pad, :] = jnp.where(line > 0, edges[3], zero)
    clean[rows + pad : rows + 2 * pad, :] = jnp.where(line < lines - 1, edges[2], zero)
    smooth(0, chans - 2)
    smooth((STEPS - 1) * chans + 2, chans - 2)
    finish(STEPS - 1)
    work(STEPS - 1)
    smooth(chans - 2, chans + 4)

    def sent(step, _):
        for copy in first_copies(step) + (relays(step) if relay else []):
            copy.wait_send()
        return 0

    lax.fori_loop(0, STEPS, sent, 0)


def local(record, slip_block, ghost_lag, order_ops):
    twins, lines = lax.axis_size("twin"), lax.axis_size("rcv")
    channels, rounds, samples = record.shape
    recs, orders = ghost_lag.shape
    groups, mine = channels // GROUP, recs * GROUP
    block = GROUP * rounds
    ways = max(twins, 4)
    far = pl.BlockSpec(memory_space=pltpu.HBM)
    smoothed = pl.pallas_call(
        functools.partial(clean_kernel, twins, lines),
        out_shape=pltpu.VMEM((channels * rounds, samples), BF16),
        in_specs=[far] * 4,
        out_specs=pl.BlockSpec(memory_space=pltpu.VMEM),
        scratch_shapes=[
            pltpu.SMEM((recs,), jnp.int32),
            pltpu.SMEM((recs, orders), jnp.int32),
            pltpu.VMEM((channels * rounds, samples), BF16),
            pltpu.VMEM((orders * samples, samples), BF16),
            pltpu.VMEM(((channels + 4) * rounds, samples), BF16),
            pltpu.VMEM((groups, twins * mine, samples), BF16),
            pltpu.VMEM((twins, 8, 128), jnp.int32),
            pltpu.VMEM((orders * block, twins * mine), BF16),
            pltpu.VMEM((2 * block, orders * samples), BF16),
            pltpu.VMEM((4, 2 * rounds, samples), BF16),
            pltpu.SemaphoreType.DMA((3,)),
            pltpu.SemaphoreType.DMA((STEPS,)),
            pltpu.SemaphoreType.DMA((twins,)),
            pltpu.SemaphoreType.DMA((twins,)),
            pltpu.SemaphoreType.DMA((STEPS, ways)),
            pltpu.SemaphoreType.DMA((STEPS, ways)),
            pltpu.SemaphoreType.DMA((2,)),
            pltpu.SemaphoreType.DMA((2,)),
        ],
        compiler_params=pltpu.CompilerParams(
            collective_id=0, has_side_effects=True, vmem_limit_bytes=56 * 2**20
        ),
        cost_estimate=pl.CostEstimate(
            flops=7 * 10**9, bytes_accessed=6 * 2**20, transcendentals=0
        ),
    )(
        slip_block, ghost_lag, record.reshape(channels * rounds, samples),
        order_ops.reshape(orders * samples, samples),
    )
    return smoothed.reshape(channels, rounds, samples)


def solution(mesh):
    placed = (P("rcv", None, "twin"), P("twin"), P("twin", None), P())
    return jax.shard_map(
        local, mesh=mesh, in_specs=placed, out_specs=P("rcv", None, "twin"), check_vma=False
    )
```

```python
import functools

import jax
import jax.numpy as jnp
from jax import lax
from jax.experimental import pallas as pl
from jax.experimental.pallas import tpu as pltpu
from jax.sharding import PartitionSpec as P

MESH = pl.DeviceIdType.MESH
GROUP = 16
STEPS = 8
AHEAD = 1
F32, BF16 = jnp.float32, jnp.bfloat16


def iota(shape, dim):
    return lax.broadcasted_iota(jnp.int32, shape, dim)


def clean_kernel(
    twins, lines, slip_hbm, lag_hbm, rec_hbm, ops_hbm, out_ref,
    slip_ref, lag_ref, rec_ref, ops_ref, clean,
    guides, lands, picks, spread, edges,
    small_sem, rec_sem, land_send, land_recv, send_sem, recv_sem, edge_send, edge_recv,
):
    me = lax.axis_index("twin")
    line = lax.axis_index("rcv")
    recs, orders = lag_ref.shape
    rows, samples = rec_ref.shape
    groups, held, _ = guides.shape
    mine = held // twins
    rounds = rows // (groups * GROUP)
    block = GROUP * rounds
    per = groups // STEPS

    def chunk(step):
        return lax.rem(step * (STEPS - 1), STEPS)

    size = rows // STEPS

    def load(step):
        part = pl.ds(pl.multiple_of(chunk(step) * size, size), size)
        return pltpu.make_async_copy(rec_hbm.at[part], rec_ref.at[part], rec_sem.at[step])

    load_slip = pltpu.make_async_copy(slip_hbm, slip_ref, small_sem.at[0])
    load_lag = pltpu.make_async_copy(lag_hbm, lag_ref, small_sem.at[1])
    load_ops = pltpu.make_async_copy(ops_hbm, ops_ref, small_sem.at[2])
    load_slip.start()
    load_lag.start()
    for step in range(STEPS):
        load(step).start()
    load_ops.start()

    others = [lax.rem(me + d, twins) for d in range(1, twins)]
    left, right = lax.rem(line + lines - 1, lines), lax.rem(line + 1, lines)
    barrier = pltpu.get_barrier_semaphore()
    for other in others:
        pl.semaphore_signal(barrier, inc=1, device_id={"twin": other}, device_id_type=MESH)
    for other in (left, right):
        pl.semaphore_signal(barrier, inc=1, device_id={"rcv": other}, device_id_type=MESH)

    load_slip.wait()
    load_lag.wait()

    order_row, rec_lane = iota((8, 128), 0), (iota((8, 128), 1) // GROUP) % recs
    land = jnp.full((8, 128), -1, jnp.int32)
    for r in range(recs):
        for h in range(orders):
            here = (order_row == h) & (rec_lane == r)
            land = jnp.where(here, slip_ref[r] - lag_ref[r, h], land)
    lands[me] = land

    row, col = iota((mine, block), 0), iota((mine, block), 1)
    slip = jnp.zeros((mine, block), jnp.int32)
    for r in range(recs):
        slip = jnp.where(row // GROUP == r, slip_ref[r], slip)
    pick = (row % GROUP == col // rounds) & ((col % rounds) * twins + me == slip)
    pick = jnp.where(pick, 1.0, 0.0).astype(BF16)

    def own(twin):
        return pl.ds(pl.multiple_of(twin * mine, mine), mine)

    def move(step, begin, count, twin, to, index):
        part = guides.at[pl.ds(chunk(step) * per + begin, count), own(twin)]
        return pltpu.make_async_remote_copy(
            src_ref=part, dst_ref=part, send_sem=send_sem.at[step, index],
            recv_sem=recv_sem.at[step, index], device_id={"twin": to}, device_id_type=MESH,
        )

    def extract(step):
        load(step).wait()

        def one(i, _):
            g = chunk(step) * per + i
            rec = rec_ref[pl.ds(pl.multiple_of(g * block, block), block), :]
            guide = jnp.dot(pick, rec, preferred_element_type=F32)
            guides[g, own(me), :] = guide.astype(BF16)
            return 0
        lax.fori_loop(0, per, one, 0)

    relay = twins == 4
    if relay:
        across = (me // 2) * 2 + (1 - me % 2)
        along = (1 - me // 2) * 2 + me % 2
        half = per // 2

    def first_copies(step):
        if relay:
            return [move(step, 0, per, me, across, 0), move(step, 0, per, me, along, 1)]
        return [move(step, 0, per, me, other, d) for d, other in enumerate(others)]

    def relays(step):
        return [
            move(step, 0, half, along, across, 2),
            move(step, half, per - half, across, along, 3),
        ]

    extract(0)
    pl.semaphore_wait(barrier, twins + 1)
    for copy in first_copies(0):
        copy.start()

    def land_copy(d):
        return pltpu.make_async_remote_copy(
            src_ref=lands.at[me], dst_ref=lands.at[me], send_sem=land_send.at[d],
            recv_sem=land_recv.at[d], device_id={"twin": others[d]}, device_id_type=MESH,
        )

    for d in range(twins - 1):
        land_copy(d).start()

    def send_next(step, _):
        extract(step)
        for copy in first_copies(step):
            copy.start()
        return 0

    def extract_next(step, _):
        extract(step)
        return 0

    lax.fori_loop(1, AHEAD, send_next, 0)
    lax.fori_loop(AHEAD, STEPS, extract_next, 0)

    for d in range(twins - 1):
        land_copy(d).wait()

    row, col = iota((block, 128), 0), iota((block, 128), 1)
    same = row // rounds == col % GROUP
    goal = (row % rounds) * twins + me
    per_tile = 128 // mine
    for tile in range(held // 128):
        for h in range(orders):
            got = lands[tile * per_tile, h : h + 1, :]
            got = jnp.broadcast_to(got, (block, 128))
            for k in range(1, per_tile):
                more = lands[tile * per_tile + k, h : h + 1, :]
                got = jnp.where(col // mine == k, jnp.broadcast_to(more, (block, 128)), got)
            hit = jnp.where(same & (got == goal), 1.0, 0.0).astype(BF16)
            picks[h * block : (h + 1) * block, tile * 128 : (tile + 1) * 128] = hit
    load_ops.wait()

    pad = 2 * rounds

    def work(step):
        def one(i, _):
            for k in range(2):
                g = chunk(step) * per + i * 2 + k
                landed = jnp.dot(picks[...], guides[g], preferred_element_type=F32).astype(BF16)
                for h in range(orders):
                    spread[k * block : (k + 1) * block, h * samples : (h + 1) * samples] = landed[
                        h * block : (h + 1) * block
                    ]
            noise = jnp.dot(spread[...], ops_ref[...], preferred_element_type=F32)
            at = (chunk(step) * per + i * 2) * block
            at = pl.multiple_of(at, 2 * block)
            rec = rec_ref[pl.ds(at, 2 * block), :].astype(F32)
            clean[pl.ds(pl.multiple_of(at + pad, pad), 2 * block), :] = (rec - noise).astype(BF16)
            return 0
        lax.fori_loop(0, per // 2, one, 0)

    def smooth(begin, count):
        at = pl.multiple_of(begin * rounds, pad)
        wide = clean[pl.ds(at, (count + 4) * rounds), :].astype(F32)
        before, middle, after = (
            wide[k * rounds : (k + count) * rounds] for k in (1, 2, 3)
        )
        out_ref[pl.ds(at, count * rounds), :] = (
            0.5 * middle + 0.25 * (before + after)
        ).astype(BF16)

    def arrive(step):
        if relay:
            for copy in first_copies(step):
                copy.wait_recv()
            for copy in relays(step):
                copy.start()

    def finish(step):
        for copy in relays(step) if relay else first_copies(step):
            copy.wait_recv()

    def edge_copies():
        return [
            pltpu.make_async_remote_copy(
                src_ref=edges.at[k], dst_ref=edges.at[2 + k], send_sem=edge_send.at[k],
                recv_sem=edge_recv.at[k], device_id={"rcv": to}, device_id_type=MESH,
            )
            for k, to in enumerate((left, right))
        ]

    chans = per * GROUP

    def window(step):
        return chunk(step) * chans + 2, chans

    def advance(step, more, ready, settled):
        arrive(step)
        if more:
            for copy in first_copies(step + AHEAD):
                copy.start()
        if ready:
            finish(step - 1)
            work(step - 1)
        if settled:
            smooth(*window(step - 1))
        return 0

    advance(0, True, False, False)
    lax.fori_loop(1, 3, lambda step, _: advance(step, True, True, False), 0)
    edges[0] = clean[pad : 2 * pad, :]
    edges[1] = clean[rows : rows + pad, :]
    for copy in edge_copies():
        copy.start()
    lax.fori_loop(3, STEPS - AHEAD, lambda step, _: advance(step, True, True, True), 0)
    lax.fori_loop(STEPS - AHEAD, STEPS, lambda step, _: advance(step, False, True, True), 0)

    for copy in edge_copies():
        copy.wait()
    zero = jnp.zeros((pad, samples), BF16)
    clean[0:pad, :] = jnp.where(line > 0, edges[3], zero)
    clean[rows + pad : rows + 2 * pad, :] = jnp.where(line < lines - 1, edges[2], zero)
    smooth(0, chans - 2)
    smooth((STEPS - 1) * chans + 2, chans - 2)
    finish(STEPS - 1)
    work(STEPS - 1)
    smooth(chans - 2, chans + 4)

    def sent(step, _):
        for copy in first_copies(step) + (relays(step) if relay else []):
            copy.wait_send()
        return 0

    lax.fori_loop(0, STEPS, sent, 0)


def local(record, slip_block, ghost_lag, order_ops):
    twins, lines = lax.axis_size("twin"), lax.axis_size("rcv")
    channels, rounds, samples = record.shape
    recs, orders = ghost_lag.shape
    groups, mine = channels // GROUP, recs * GROUP
    block = GROUP * rounds
    ways = max(twins, 4)
    far = pl.BlockSpec(memory_space=pltpu.HBM)
    smoothed = pl.pallas_call(
        functools.partial(clean_kernel, twins, lines),
        out_shape=pltpu.VMEM((channels * rounds, samples), BF16),
        in_specs=[far] * 4,
        out_specs=pl.BlockSpec(memory_space=pltpu.VMEM),
        scratch_shapes=[
            pltpu.SMEM((recs,), jnp.int32),
            pltpu.SMEM((recs, orders), jnp.int32),
            pltpu.VMEM((channels * rounds, samples), BF16),
            pltpu.VMEM((orders * samples, samples), BF16),
            pltpu.VMEM(((channels + 4) * rounds, samples), BF16),
            pltpu.VMEM((groups, twins * mine, samples), BF16),
            pltpu.VMEM((twins, 8, 128), jnp.int32),
            pltpu.VMEM((orders * block, twins * mine), BF16),
            pltpu.VMEM((2 * block, orders * samples), BF16),
            pltpu.VMEM((4, 2 * rounds, samples), BF16),
            pltpu.SemaphoreType.DMA((3,)),
            pltpu.SemaphoreType.DMA((STEPS,)),
            pltpu.SemaphoreType.DMA((twins,)),
            pltpu.SemaphoreType.DMA((twins,)),
            pltpu.SemaphoreType.DMA((STEPS, ways)),
            pltpu.SemaphoreType.DMA((STEPS, ways)),
            pltpu.SemaphoreType.DMA((2,)),
            pltpu.SemaphoreType.DMA((2,)),
        ],
        compiler_params=pltpu.CompilerParams(
            collective_id=0, has_side_effects=True, vmem_limit_bytes=56 * 2**20
        ),
        cost_estimate=pl.CostEstimate(
            flops=7 * 10**9, bytes_accessed=6 * 2**20, transcendentals=0
        ),
    )(
        slip_block, ghost_lag, record.reshape(channels * rounds, samples),
        order_ops.reshape(orders * samples, samples),
    )
    return smoothed.reshape(channels, rounds, samples)


def solution(mesh):
    placed = (P("rcv", None, "twin"), P("twin"), P("twin", None), P())
    return jax.shard_map(
        local, mesh=mesh, in_specs=placed, out_specs=P("rcv", None, "twin"), check_vma=False
    )
```
